32 devices in a mesh: sub: 4 (over z), row: 2 (over x), col: 4 (over y, core).
Axes of the slice: x: 2, y: 2, z: 4, core: 2. Of those that a mesh axis runs over, the one named last changes fastest.
Arguments:
- front_in: float32 [12288, 12288], P('row', ('sub', 'col')), as said below
- child_updates: float32 [4, 8192, 8192], P('sub', 'row', 'col'), as said below
- pattern: int32 [4, 32, 32], P('sub', 'row', 'col'), may hold values from 0 to 1, as said below
- child_map: int32 [4, 32], replicated, may hold values from 0 to 47, as said below
- pivot_inverse: float32 [1024, 1024], replicated, as said below
Outputs:
- front_out: float32 [12288, 12288], P('row', ('sub', 'col'))
The draws below stay inside these ranges and needn't reach their ends.
Inputs may be any that keep to these rules, and one draw needn't show every extreme that they name: front_in is symmetric. Each child_updates[s] is symmetric. Each pattern[s] is symmetric. child_map[s] is strictly increasing, and child_map[s, i] // 3 equals i // 2. pivot_inverse is lower triangular with a positive diagonal.
All inputs are finite; a program needn't handle non-finite values.
Results may differ from the reference program's by a relative error of at most 0.000053.
Values sent between devices are 32-bit elements; how exact they have to be, the bound alone decides.
A program may use at most 256 MiB of HBM per device.

```python
import jax
import jax.numpy as jnp
from jax import lax

BLK = 256
FRONT = 12288
CHILD = 8192
PANEL = 1024
GROUPS = 16
CHILDREN = 4
FBLOCKS = 48
CBLOCKS = 32


def symmetric_field(key, shape):
    first = jax.random.fold_in(key, 0)
    base = jnp.clip(jax.random.normal(first, shape, dtype=jnp.float32), -6.0, 6.0)
    return ((base + jnp.swapaxes(base, -1, -2)) * 0.70710678).astype(jnp.float32)


def draw_front_in(key, part):
    field = symmetric_field(jax.random.fold_in(key, 11), (FRONT, FRONT))
    return field.astype(jnp.float32)


def draw_child_updates(key, part):
    return symmetric_field(jax.random.fold_in(key, 21), (CHILDREN, CHILD, CHILD))


def draw_pattern(key, part):
    levels = jax.random.randint(jax.random.fold_in(key, 31), (CHILDREN, CBLOCKS, CBLOCKS), 0, 4)
    upper = (levels < 3).astype(jnp.int32)
    rows_idx = jnp.arange(CBLOCKS)[:, None]
    cols_idx = jnp.arange(CBLOCKS)[None, :]
    return jnp.where((rows_idx <= cols_idx)[None], upper, jnp.swapaxes(upper, 1, 2)).astype(jnp.int32)


def draw_child_map(key, part):
    fgroup = FBLOCKS // GROUPS
    cgroup = CBLOCKS // GROUPS
    omitted = jax.random.randint(key, (CHILDREN, GROUPS), 0, fgroup)
    omitted = omitted.at[0, 0].set(fgroup - 1).at[0, GROUPS - 1].set(0)
    slots = jnp.arange(cgroup, dtype=jnp.int32)
    chosen = slots[None, None, :] + (slots[None, None, :] >= omitted[:, :, None]).astype(jnp.int32)
    starts = (jnp.arange(GROUPS, dtype=jnp.int32) * fgroup)[None, :, None]
    return (starts + chosen).reshape(CHILDREN, CBLOCKS).astype(jnp.int32)


def draw_pivot_inverse(key, part):
    first, second = jax.random.split(key, 2)
    offdiag = 0.006 * jax.random.normal(first, (PANEL, PANEL), dtype=jnp.float32)
    diagonal = jnp.exp(jax.random.uniform(second, (PANEL,), minval=jnp.log(0.1), maxval=jnp.log(0.2)))
    rows_idx = jnp.arange(PANEL)[:, None]
    cols_idx = jnp.arange(PANEL)[None, :]
    strict = jnp.where(rows_idx > cols_idx, offdiag, 0.0)
    return (strict + jnp.where(rows_idx == cols_idx, diagonal[:, None], 0.0)).astype(jnp.float32)


def setup_inputs(seed: int = 0) -> dict:
    seeds = jax.random.split(jax.random.key(seed), 6)
    front_in = draw_front_in(jax.random.fold_in(seeds[5], 71), 0)
    child_updates = draw_child_updates(jax.random.fold_in(seeds[5], 71), 0)
    pattern = draw_pattern(jax.random.fold_in(seeds[5], 71), 0)
    child_map = draw_child_map(jax.random.fold_in(seeds[5], 71), 0)
    pivot_inverse = draw_pivot_inverse(jax.random.fold_in(seeds[5], 71), 0)
    return {"front_in": front_in, "child_updates": child_updates, "pattern": pattern, "child_map": child_map, "pivot_inverse": pivot_inverse}


def reference(front_in, child_updates, pattern, child_map, pivot_inverse):
    fblocks = FRONT // BLK
    cblocks = CHILD // BLK
    blocks = front_in.reshape(fblocks, BLK, fblocks, BLK).transpose(0, 2, 1, 3)
    for source in range(CHILDREN):
        update = child_updates[source].reshape(cblocks, BLK, cblocks, BLK).transpose(0, 2, 1, 3)
        update = update * pattern[source][:, :, None, None].astype(jnp.float32)
        targets = child_map[source]
        blocks = blocks.at[targets[:, None], targets[None, :]].add(update)
    assembled = blocks.transpose(0, 2, 1, 3).reshape(FRONT, FRONT)
    factor = jnp.dot(assembled[PANEL:, :PANEL], pivot_inverse.T, precision=lax.Precision.HIGHEST, preferred_element_type=jnp.float32)
    trailing = assembled[PANEL:, PANEL:] - jnp.dot(factor, factor.T, precision=lax.Precision.HIGHEST, preferred_element_type=jnp.float32)
    return assembled.at[PANEL:, :PANEL].set(factor).at[PANEL:, PANEL:].set(trailing)
```

```python
import functools

import jax
import jax.numpy as jnp
from jax import lax
from jax.experimental import pallas as pl
from jax.experimental.pallas import tpu as pltpu
from jax.sharding import PartitionSpec as P

BLK = 256
FRONT = 12288
CHILD = 8192
PANEL = 1024
MESH = pl.DeviceIdType.MESH


def exchange_kernel(count, first, rows, chunks, aliased, *refs):
    if aliased:
        child, _, stage, out = refs[:4]
        send1, recv1, send2, recv2 = refs[4:]
    else:
        child, stage, out = refs[:3]
        send1, recv1, send2, recv2 = refs[3:]
    sub = lax.axis_index("sub")
    row = lax.axis_index("row")
    col = lax.axis_index("col")
    width = out.shape[2]
    size = rows // chunks

    barrier = pltpu.get_barrier_semaphore()
    for step in range(1, count):
        pl.semaphore_signal(
            barrier, inc=1, device_id=(sub, row, lax.rem(col + step, count)), device_id_type=MESH
        )
        pl.semaphore_signal(
            barrier, inc=1, device_id=(lax.rem(sub + step, count), row, col), device_id_type=MESH
        )
    pl.semaphore_wait(barrier, 2 * (count - 1))

    def columns(index):
        return pl.ds(pl.multiple_of(index * width, width), width)

    def spread(part, step):
        target = lax.rem(col + step, count)
        return pltpu.make_async_remote_copy(
            src_ref=child.at[0, pl.ds(first + part * size, size), columns(target)],
            dst_ref=stage.at[col, pl.ds(part * size, size), :],
            send_sem=send1.at[part, step],
            recv_sem=recv1.at[part, col],
            device_id=(sub, row, target),
            device_id_type=MESH,
        )

    def keep(part):
        return pltpu.make_async_copy(
            child.at[0, pl.ds(first + part * size, size), columns(col)],
            stage.at[col, pl.ds(part * size, size), :],
            recv1.at[part, col],
        )

    def deliver(part, step):
        target = lax.rem(sub + step, count)
        return pltpu.make_async_remote_copy(
            src_ref=stage.at[target, pl.ds(part * size, size), :],
            dst_ref=out.at[sub, pl.ds(first + part * size, size), :],
            send_sem=send2.at[part, step],
            recv_sem=recv2.at[part, sub],
            device_id=(target, row, col),
            device_id_type=MESH,
        )

    def place(part):
        return pltpu.make_async_copy(
            stage.at[sub, pl.ds(part * size, size), :],
            out.at[sub, pl.ds(first + part * size, size), :],
            recv2.at[part, sub],
        )

    def arrived(ref, sem):
        pltpu.make_async_copy(ref, ref, sem).wait()

    for part in range(chunks):
        for step in range(1, count):
            spread(part, step).start()
        keep(part).start()
    for part in range(chunks):
        for step in list(range(1, count)) + [0]:
            source = lax.rem(sub + step, count)
            arrived(stage.at[source, pl.ds(part * size, size), :], recv1.at[part, source])
            if step:
                deliver(part, step).start()
            else:
                place(part).start()
    for part in range(chunks):
        for source in range(count):
            arrived(out.at[source, pl.ds(first + part * size, size), :], recv2.at[part, source])
        for step in range(1, count):
            spread(part, step).wait_send()
            deliver(part, step).wait_send()


def exchange(child, received, first, rows, chunks, count, ident):
    total, width = child.shape[1], child.shape[2] // count
    aliased = received is not None
    operands = (child, received) if aliased else (child,)
    anywhere = pl.BlockSpec(memory_space=pl.ANY)
    moved = 2 * count * rows * width * 4
    _, result = pl.pallas_call(
        functools.partial(exchange_kernel, count, first, rows, chunks, aliased),
        out_shape=[
            jax.ShapeDtypeStruct((count, rows, width), jnp.float32),
            jax.ShapeDtypeStruct((count, total, width), jnp.float32),
        ],
        in_specs=[anywhere] * len(operands),
        out_specs=[anywhere, anywhere],
        scratch_shapes=[pltpu.SemaphoreType.DMA((chunks, count))] * 4,
        input_output_aliases={1: 1} if aliased else {},
        compiler_params=pltpu.CompilerParams(
            collective_id=ident, has_side_effects=True, vmem_limit_bytes=48 * 2**20
        ),
        cost_estimate=pl.CostEstimate(flops=0, bytes_accessed=40 * moved, transcendentals=0),
    )(*operands)
    return result


def extended_columns(weights, a, front, pieces, column):
    total = front[:, column * BLK : (column + 1) * BLK]
    for s, piece in enumerate(pieces):
        for j in range(2):
            weight = weights[((a * len(pieces) + s) * 3 + column) * 2 + j]
            total = total + weight * piece[0, :, j * BLK : (j + 1) * BLK]
    return total


def strip_kernel(count, where, weights, front, *refs):
    a = pl.program_id(0)
    for column in range(3):
        refs[-1][:, column * BLK : (column + 1) * BLK] = extended_columns(
            weights, a, front, refs[:count], column
        )


def final_kernel(count, panel_blocks, where, weights, front, *refs):
    pieces = refs[:count]
    rows_factor, cols_factor, out, high, low = refs[count:]
    a = pl.program_id(0)
    row_block = where[0] + a
    contract = (((1,), (1,)), ((), ()))

    @pl.when(a == 0)
    def _():
        value = cols_factor[...]
        top = value.astype(jnp.bfloat16)
        high[...] = top
        low[...] = (value - top.astype(jnp.float32)).astype(jnp.bfloat16)

    value = rows_factor[...]
    top = value.astype(jnp.bfloat16)
    rest = (value - top.astype(jnp.float32)).astype(jnp.bfloat16)
    for column in range(3):
        col_block = where[1] + column
        span = slice(column * BLK, (column + 1) * BLK)
        here = extended_columns(weights, a, front, pieces, column)
        dot = functools.partial(
            lax.dot_general, dimension_numbers=contract, preferred_element_type=jnp.float32
        )
        update = dot(top, low[span, :]) + dot(rest, high[span, :]) + dot(top, high[span, :])
        both = jnp.logical_and(row_block >= panel_blocks, col_block >= panel_blocks)
        out[:, span] = jnp.where(both, here - update, here)

        @pl.when(jnp.logical_and(row_block >= panel_blocks, col_block < panel_blocks))
        def _():
            source = jnp.minimum(col_block, panel_blocks - 1) * BLK
            out[:, span] = rows_factor[:, pl.ds(pl.multiple_of(source, BLK), BLK)]


def piece_specs(count, offset):
    def one(s):
        return pl.BlockSpec((1, BLK, 2 * BLK), lambda a, where: (s, where[offset + a * count + s], 0))

    return [one(s) for s in range(count)]


def shards(front_in, child_updates, pattern, child_map, pivot_inverse):
    sub_count = lax.axis_size("sub")
    row_count = lax.axis_size("row")
    col_count = lax.axis_size("col")
    assert sub_count == col_count
    count = sub_count
    groups = sub_count * col_count
    row_id = lax.axis_index("row")
    group_id = lax.axis_index("sub") * col_count + lax.axis_index("col")
    row_blocks = FRONT // BLK // row_count
    col_blocks = FRONT // BLK // groups
    child_rows = CHILD // BLK // row_count
    child_cols = CHILD // BLK // groups
    panel_blocks = PANEL // BLK
    group_cols = col_blocks * BLK
    first_row = row_id * row_blocks
    first_col = group_id * col_blocks
    assert col_blocks == 3 and child_cols == 2

    masks = lax.all_gather(pattern[0], ("sub", "col"), axis=0, tiled=False)
    masks = masks.reshape(sub_count, col_count, child_rows, CHILD // BLK // col_count)
    masks = masks.transpose(0, 2, 1, 3).reshape(sub_count, child_rows, CHILD // BLK)
    mine = lax.dynamic_slice_in_dim(masks, group_id * child_cols, child_cols, 2)
    rows_map = lax.dynamic_slice_in_dim(child_map, row_id * child_rows, child_rows, 1)
    cols_map = lax.dynamic_slice_in_dim(child_map, group_id * child_cols, child_cols, 1)
    row_at = first_row + jnp.arange(row_blocks, dtype=jnp.int32)
    col_at = first_col + jnp.arange(col_blocks, dtype=jnp.int32)
    row_hit = rows_map[None] == row_at[:, None, None]
    col_hit = cols_map[None] == col_at[:, None, None]
    fallback = (jnp.arange(row_blocks, dtype=jnp.int32) // 3 * 2)[:, None]
    indices = jnp.arange(child_rows, dtype=jnp.int32)
    row_from = jnp.where(
        row_hit.any(2), jnp.sum(jnp.where(row_hit, indices, 0), axis=2), fallback
    ).astype(jnp.int32)
    kept = jnp.sum(jnp.where(row_hit[..., None], mine[None], 0), axis=2)
    weights = jnp.where(col_hit[None], kept.transpose(0, 1, 2)[:, None], 0)
    weights = weights.transpose(0, 2, 1, 3).astype(jnp.float32).reshape(-1)
    where = jnp.concatenate(
        [jnp.stack([first_row, first_col]).astype(jnp.int32), row_from.reshape(-1)]
    )

    rows = child_rows * BLK
    head = min(rows, 4 * BLK)
    received = exchange(child_updates, None, 0, head, 2, count, 0)
    strip_blocks = min(panel_blocks, row_blocks)
    smem = pl.BlockSpec(memory_space=pltpu.SMEM)
    front_spec = pl.BlockSpec((BLK, group_cols), lambda a, where: (a, 0))
    strip = pl.pallas_call(
        functools.partial(strip_kernel, count),
        grid_spec=pltpu.PrefetchScalarGridSpec(
            num_scalar_prefetch=1,
            grid=(strip_blocks,),
            in_specs=[smem, front_spec] + piece_specs(count, 2),
            out_specs=front_spec,
        ),
        out_shape=jax.ShapeDtypeStruct((strip_blocks * BLK, group_cols), jnp.float32),
        cost_estimate=pl.CostEstimate(flops=0, bytes_accessed=20 * 2**20, transcendentals=0),
    )(where, weights, front_in, *([received] * count))
    if row_count == 1:
        panel_t = strip
    elif row_count == 2 and strip_blocks == panel_blocks:
        other = lax.ppermute(strip, "row", [(0, 1)])
        panel_t = jnp.where(row_id == 0, strip, other)
    else:
        span = strip_blocks * BLK
        parts = -(-PANEL // span)
        pieces = [jnp.where(row_id == part, strip, 0.0) for part in range(parts)]
        panel_t = lax.psum(jnp.concatenate(pieces, axis=0)[:PANEL], "row")
    cols_factor = lax.dot_general(
        panel_t,
        pivot_inverse,
        (((0,), (1,)), ((), ())),
        precision=lax.Precision.HIGHEST,
        preferred_element_type=jnp.float32,
    )

    group_rows = groups // row_count
    left = rows - head
    if left:
        child, cols_factor = lax.optimization_barrier((child_updates, cols_factor))
        half = left // 2
        received = exchange(child, received, head, half, 3, count, 1)
    if group_rows >= col_count:
        deep = group_rows // col_count
        along = lax.all_gather(cols_factor, "sub", axis=0, tiled=False)
        if left:
            along, received = lax.optimization_barrier((along, received))
        needed = lax.dynamic_slice_in_dim(along, row_id * deep, deep, 0)
        if left:
            child, needed = lax.optimization_barrier((child, needed))
        gathered = lax.all_gather(needed, "col", axis=0, tiled=False)
        gathered = gathered.reshape(-1, PANEL)

        def factor_at(a, where):
            group = a // 3
            return ((group % col_count) * deep + group // col_count) * 3 + a % 3, 0
    else:
        gathered = lax.all_gather(cols_factor, ("sub", "col"), axis=0, tiled=False)
        gathered = lax.dynamic_slice_in_dim(gathered, row_id * group_rows, group_rows, 0)
        gathered = gathered.reshape(-1, PANEL)

        def factor_at(a, where):
            return a, 0

    if left:
        received = exchange(child, received, head + half, left - half, 3, count, 2)
    return pl.pallas_call(
        functools.partial(final_kernel, count, panel_blocks),
        grid_spec=pltpu.PrefetchScalarGridSpec(
            num_scalar_prefetch=1,
            grid=(row_blocks,),
            in_specs=[smem, front_spec]
            + piece_specs(count, 2)
            + [
                pl.BlockSpec((BLK, PANEL), factor_at),
                pl.BlockSpec((group_cols, PANEL), lambda a, where: (0, 0)),
            ],
            out_specs=front_spec,
            scratch_shapes=[pltpu.VMEM((group_cols, PANEL), jnp.bfloat16)] * 2,
        ),
        out_shape=jax.ShapeDtypeStruct((row_blocks * BLK, group_cols), jnp.float32),
        compiler_params=pltpu.CompilerParams(vmem_limit_bytes=48 * 2**20),
        cost_estimate=pl.CostEstimate(
            flops=6 * row_blocks * BLK * group_cols * PANEL,
            bytes_accessed=100 * 2**20,
            transcendentals=0,
        ),
    )(where, weights, front_in, *([received] * count), gathered, cols_factor)


def solution(mesh):
    in_specs = (P("row", ("sub", "col")), P("sub", "row", "col"), P("sub", "row", "col"), P(), P())
    out_specs = P("row", ("sub", "col"))
    return jax.shard_map(shards, mesh=mesh, in_specs=in_specs, out_specs=out_specs, check_vma=False)
```

```python
import functools

import jax
import jax.numpy as jnp
from jax import lax
from jax.experimental import pallas as pl
from jax.experimental.pallas import tpu as pltpu
from jax.sharding import PartitionSpec as P

BLK = 256
FRONT = 12288
CHILD = 8192
PANEL = 1024
MESH = pl.DeviceIdType.MESH


def exchange_kernel(count, first, rows, chunks, aliased, *refs):
    if aliased:
        child, _, stage, out = refs[:4]
        send1, recv1, send2, recv2 = refs[4:]
    else:
        child, stage, out = refs[:3]
        send1, recv1, send2, recv2 = refs[3:]
    sub = lax.axis_index("sub")
    row = lax.axis_index("row")
    col = lax.axis_index("col")
    width = out.shape[2]
    size = rows // chunks

    barrier = pltpu.get_barrier_semaphore()
    for step in range(1, count):
        pl.semaphore_signal(
            barrier, inc=1, device_id=(sub, row, lax.rem(col + step, count)), device_id_type=MESH
        )
        pl.semaphore_signal(
            barrier, inc=1, device_id=(lax.rem(sub + step, count), row, col), device_id_type=MESH
        )
    pl.semaphore_wait(barrier, 2 * (count - 1))

    def columns(index):
        return pl.ds(pl.multiple_of(index * width, width), width)

    def spread(part, step):
        target = lax.rem(col + step, count)
        return pltpu.make_async_remote_copy(
            src_ref=child.at[0, pl.ds(first + part * size, size), columns(target)],
            dst_ref=stage.at[col, pl.ds(part * size, size), :],
            send_sem=send1.at[part, step],
            recv_sem=recv1.at[part, col],
            device_id=(sub, row, target),
            device_id_type=MESH,
        )

    def keep(part):
        return pltpu.make_async_copy(
            child.at[0, pl.ds(first + part * size, size), columns(col)],
            stage.at[col, pl.ds(part * size, size), :],
            recv1.at[part, col],
        )

    def deliver(part, step):
        target = lax.rem(sub + step, count)
        return pltpu.make_async_remote_copy(
            src_ref=stage.at[target, pl.ds(part * size, size), :],
            dst_ref=out.at[sub, pl.ds(first + part * size, size), :],
            send_sem=send2.at[part, step],
            recv_sem=recv2.at[part, sub],
            device_id=(target, row, col),
            device_id_type=MESH,
        )

    def place(part):
        return pltpu.make_async_copy(
            stage.at[sub, pl.ds(part * size, size), :],
            out.at[sub, pl.ds(first + part * size, size), :],
            recv2.at[part, sub],
        )

    def arrived(ref, sem):
        pltpu.make_async_copy(ref, ref, sem).wait()

    for part in range(chunks):
        for step in range(1, count):
            spread(part, step).start()
        keep(part).start()
    for part in range(chunks):
        for step in list(range(1, count)) + [0]:
            source = lax.rem(sub + step, count)
            arrived(stage.at[source, pl.ds(part * size, size), :], recv1.at[part, source])
            if step:
                deliver(part, step).start()
            else:
                place(part).start()
    for part in range(chunks):
        for source in range(count):
            arrived(out.at[source, pl.ds(first + part * size, size), :], recv2.at[part, source])
        for step in range(1, count):
            spread(part, step).wait_send()
            deliver(part, step).wait_send()


def exchange(child, received, first, rows, chunks, count, ident):
    total, width = child.shape[1], child.shape[2] // count
    aliased = received is not None
    operands = (child, received) if aliased else (child,)
    anywhere = pl.BlockSpec(memory_space=pl.ANY)
    moved = 2 * count * rows * width * 4
    _, result = pl.pallas_call(
        functools.partial(exchange_kernel, count, first, rows, chunks, aliased),
        out_shape=[
            jax.ShapeDtypeStruct((count, rows, width), jnp.float32),
            jax.ShapeDtypeStruct((count, total, width), jnp.float32),
        ],
        in_specs=[anywhere] * len(operands),
        out_specs=[anywhere, anywhere],
        scratch_shapes=[pltpu.SemaphoreType.DMA((chunks, count))] * 4,
        input_output_aliases={1: 1} if aliased else {},
        compiler_params=pltpu.CompilerParams(
            collective_id=ident, has_side_effects=True, vmem_limit_bytes=48 * 2**20
        ),
        cost_estimate=pl.CostEstimate(flops=0, bytes_accessed=40 * moved, transcendentals=0),
    )(*operands)
    return result


def extended_columns(weights, a, front, pieces, column):
    total = front[:, column * BLK : (column + 1) * BLK]
    for s, piece in enumerate(pieces):
        for j in range(2):
            weight = weights[((a * len(pieces) + s) * 3 + column) * 2 + j]
            total = total + weight * piece[0, :, j * BLK : (j + 1) * BLK]
    return total


def strip_kernel(count, where, weights, front, *refs):
    a = pl.program_id(0)
    for column in range(3):
        refs[-1][:, column * BLK : (column + 1) * BLK] = extended_columns(
            weights, a, front, refs[:count], column
        )


def final_kernel(count, panel_blocks, where, weights, front, *refs):
    pieces = refs[:count]
    rows_first, rows_second, cols_factor, out, right, rows_factor = refs[count:]
    a = pl.program_id(0)
    row_block = where[0] + a

    def split(value):
        top = value.astype(jnp.bfloat16)
        return top, (value - top.astype(jnp.float32)).astype(jnp.bfloat16)

    @pl.when(a == 0)
    def _():
        top, rest = split(cols_factor[...])
        right[:, :PANEL] = rest
        right[:, PANEL : 2 * PANEL] = top
        right[:, 2 * PANEL :] = top

    rows_factor[:, : PANEL // 2] = rows_first[...]
    rows_factor[:, PANEL // 2 :] = rows_second[...]
    top, rest = split(rows_factor[...])
    left = jnp.concatenate([top, rest, top], axis=1)
    for column in range(3):
        col_block = where[1] + column
        span = slice(column * BLK, (column + 1) * BLK)
        here = extended_columns(weights, a, front, pieces, column)
        update = lax.dot_general(
            left, right[span, :], (((1,), (1,)), ((), ())), preferred_element_type=jnp.float32
        )
        both = jnp.logical_and(row_block >= panel_blocks, col_block >= panel_blocks)
        out[:, span] = jnp.where(both, here - update, here)

        @pl.when(jnp.logical_and(row_block >= panel_blocks, col_block < panel_blocks))
        def _():
            source = jnp.minimum(col_block, panel_blocks - 1) * BLK
            out[:, span] = rows_factor[:, pl.ds(pl.multiple_of(source, BLK), BLK)]


def piece_specs(count, offset):
    def one(s):
        return pl.BlockSpec((1, BLK, 2 * BLK), lambda a, where: (s, where[offset + a * count + s], 0))

    return [one(s) for s in range(count)]


def column_factor(panel_t, pivot_inverse):
    return lax.dot_general(
        panel_t,
        pivot_inverse,
        (((0,), (1,)), ((), ())),
        precision=lax.Precision.HIGH,
        preferred_element_type=jnp.float32,
    )


def shards(front_in, child_updates, pattern, child_map, pivot_inverse):
    sub_count = lax.axis_size("sub")
    row_count = lax.axis_size("row")
    col_count = lax.axis_size("col")
    assert sub_count == col_count
    count = sub_count
    groups = sub_count * col_count
    row_id = lax.axis_index("row")
    group_id = lax.axis_index("sub") * col_count + lax.axis_index("col")
    row_blocks = FRONT // BLK // row_count
    col_blocks = FRONT // BLK // groups
    child_rows = CHILD // BLK // row_count
    child_cols = CHILD // BLK // groups
    panel_blocks = PANEL // BLK
    group_cols = col_blocks * BLK
    first_row = row_id * row_blocks
    first_col = group_id * col_blocks
    assert col_blocks == 3 and child_cols == 2

    masks = lax.all_gather(pattern[0].astype(jnp.float32), ("sub", "col"), axis=0, tiled=False)
    masks = masks.reshape(sub_count, col_count, child_rows, CHILD // BLK // col_count)
    masks = masks.transpose(0, 2, 1, 3).reshape(sub_count, child_rows, CHILD // BLK)
    mine = lax.dynamic_slice_in_dim(masks, group_id * child_cols, child_cols, 2)
    rows_map = lax.dynamic_slice_in_dim(child_map, row_id * child_rows, child_rows, 1)
    cols_map = lax.dynamic_slice_in_dim(child_map, group_id * child_cols, child_cols, 1)
    row_at = first_row + jnp.arange(row_blocks, dtype=jnp.int32)
    col_at = first_col + jnp.arange(col_blocks, dtype=jnp.int32)
    row_hit = rows_map[None] == row_at[:, None, None]
    col_hit = cols_map[None] == col_at[:, None, None]
    fallback = (jnp.arange(row_blocks, dtype=jnp.int32) // 3 * 2)[:, None]
    indices = jnp.arange(child_rows, dtype=jnp.int32)
    row_from = jnp.where(
        row_hit.any(2), jnp.sum(jnp.where(row_hit, indices, 0), axis=2), fallback
    ).astype(jnp.int32)
    kept = jnp.sum(jnp.where(row_hit[..., None], mine[None], 0.0), axis=2)
    weights = jnp.where(col_hit[None], kept[:, None], 0.0)
    weights = weights.transpose(0, 2, 1, 3).reshape(-1)
    where = jnp.concatenate(
        [jnp.stack([first_row, first_col]).astype(jnp.int32), row_from.reshape(-1)]
    )

    rows = child_rows * BLK
    head = min(rows, 4 * BLK)
    received = exchange(child_updates, None, 0, head, head // BLK, count, 0)
    strip_blocks = min(panel_blocks, row_blocks)
    smem = pl.BlockSpec(memory_space=pltpu.SMEM)
    front_spec = pl.BlockSpec((BLK, group_cols), lambda a, where: (a, 0))
    strip = pl.pallas_call(
        functools.partial(strip_kernel, count),
        grid_spec=pltpu.PrefetchScalarGridSpec(
            num_scalar_prefetch=1,
            grid=(strip_blocks,),
            in_specs=[smem, front_spec] + piece_specs(count, 2),
            out_specs=front_spec,
        ),
        out_shape=jax.ShapeDtypeStruct((strip_blocks * BLK, group_cols), jnp.float32),
        cost_estimate=pl.CostEstimate(flops=0, bytes_accessed=20 * 2**20, transcendentals=0),
    )(where, weights, front_in, *([received] * count))
    group_rows = groups // row_count
    left = rows - head
    child = child_updates
    done = head

    def more(received, blocks, ident):
        return exchange(child, received, done, blocks * BLK, blocks, count, ident)

    if row_count == 2 and strip_blocks == panel_blocks:
        parts = (2, 3, 3, left // BLK - 8)
        child, strip = lax.optimization_barrier((child, strip))
        other = lax.ppermute(strip, "row", [(0, 1)])
        received = more(received, parts[0], 1)
        done += parts[0] * BLK
        other, received = lax.optimization_barrier((other, received))
        cols_factor = column_factor(jnp.where(row_id == 0, strip, other), pivot_inverse)

        deep = group_rows // col_count
        wide = PANEL // 2
        half = (lax.axis_index("sub") // deep != row_id).astype(jnp.int32)
        sent = lax.dynamic_slice_in_dim(cols_factor, half * wide, wide, 1)
        child, sent = lax.optimization_barrier((child, sent))
        along = lax.all_gather(sent, "sub", axis=0, tiled=False)
        received = more(received, parts[1], 2)
        done += parts[1] * BLK
        along, received = lax.optimization_barrier((along, received))

        first = lax.dynamic_slice_in_dim(along, row_id * deep, deep, 0)
        passed = lax.dynamic_slice_in_dim(along, (1 - row_id) * deep, deep, 0)
        child, first, passed = lax.optimization_barrier((child, first, passed))
        second = lax.ppermute(passed, "row", [(0, 1), (1, 0)])
        first = lax.all_gather(first, "col", axis=0, tiled=False).reshape(-1, wide)
        received = more(received, parts[2], 3)
        done += parts[2] * BLK
        second, received = lax.optimization_barrier((second, received))

        child, second = lax.optimization_barrier((child, second))
        second = lax.all_gather(second, "col", axis=0, tiled=False).reshape(-1, wide)
        received = more(received, parts[3], 4)

        def factor_at(a):
            group = a // 3
            return ((group % col_count) * deep + group // col_count) * 3 + a % 3

        second_at = 0
    else:
        if left:
            received = more(received, left // BLK, 1)
        span = strip_blocks * BLK
        pieces = [jnp.where(row_id == part, strip, 0.0) for part in range(-(-PANEL // span))]
        panel_t = lax.psum(jnp.concatenate(pieces, axis=0)[:PANEL], "row")
        cols_factor = column_factor(panel_t, pivot_inverse)
        gathered = lax.all_gather(cols_factor, ("sub", "col"), axis=0, tiled=False)
        gathered = lax.dynamic_slice_in_dim(gathered, row_id * group_rows, group_rows, 0)
        first = second = gathered.reshape(-1, PANEL)

        def factor_at(a):
            return a

        second_at = 1

    return pl.pallas_call(
        functools.partial(final_kernel, count, panel_blocks),
        grid_spec=pltpu.PrefetchScalarGridSpec(
            num_scalar_prefetch=1,
            grid=(row_blocks,),
            in_specs=[smem, front_spec]
            + piece_specs(count, 2)
            + [
                pl.BlockSpec((BLK, PANEL // 2), lambda a, where: (factor_at(a), 0)),
                pl.BlockSpec((BLK, PANEL // 2), lambda a, where: (factor_at(a), second_at)),
                pl.BlockSpec((group_cols, PANEL), lambda a, where: (0, 0)),
            ],
            out_specs=front_spec,
            scratch_shapes=[
                pltpu.VMEM((group_cols, 3 * PANEL), jnp.bfloat16),
                pltpu.VMEM((BLK, PANEL), jnp.float32),
            ],
        ),
        out_shape=jax.ShapeDtypeStruct((row_blocks * BLK, group_cols), jnp.float32),
        compiler_params=pltpu.CompilerParams(vmem_limit_bytes=48 * 2**20),
        cost_estimate=pl.CostEstimate(
            flops=6 * row_blocks * BLK * group_cols * PANEL,
            bytes_accessed=100 * 2**20,
            transcendentals=0,
        ),
    )(where, weights, front_in, *([received] * count), first, second, cols_factor)


def solution(mesh):
    in_specs = (P("row", ("sub", "col")), P("sub", "row", "col"), P("sub", "row", "col"), P(), P())
    out_specs = P("row", ("sub", "col"))
    return jax.shard_map(shards, mesh=mesh, in_specs=in_specs, out_specs=out_specs, check_vma=False)
```

```python
import functools

import jax
import jax.numpy as jnp
from jax import lax
from jax.experimental import pallas as pl
from jax.experimental.pallas import tpu as pltpu
from jax.sharding import PartitionSpec as P

BLK = 256
FRONT = 12288
CHILD = 8192
PANEL = 1024
MESH = pl.DeviceIdType.MESH


def exchange_kernel(count, first, rows, chunks, aliased, *refs):
    if aliased:
        child, _, stage, out = refs[:4]
        send1, recv1, send2, recv2 = refs[4:]
    else:
        child, stage, out = refs[:3]
        send1, recv1, send2, recv2 = refs[3:]
    sub = lax.axis_index("sub")
    row = lax.axis_index("row")
    col = lax.axis_index("col")
    width = out.shape[2]
    size = rows // chunks

    barrier = pltpu.get_barrier_semaphore()
    for step in range(1, count):
        pl.semaphore_signal(
            barrier, inc=1, device_id=(sub, row, lax.rem(col + step, count)), device_id_type=MESH
        )
        pl.semaphore_signal(
            barrier, inc=1, device_id=(lax.rem(sub + step, count), row, col), device_id_type=MESH
        )
    pl.semaphore_wait(barrier, 2 * (count - 1))

    def columns(index):
        return pl.ds(pl.multiple_of(index * width, width), width)

    def spread(part, step):
        target = lax.rem(col + step, count)
        return pltpu.make_async_remote_copy(
            src_ref=child.at[0, pl.ds(first + part * size, size), columns(target)],
            dst_ref=stage.at[col, pl.ds(part * size, size), :],
            send_sem=send1.at[part, step],
            recv_sem=recv1.at[part, col],
            device_id=(sub, row, target),
            device_id_type=MESH,
        )

    def keep(part):
        return pltpu.make_async_copy(
            child.at[0, pl.ds(first + part * size, size), columns(col)],
            stage.at[col, pl.ds(part * size, size), :],
            recv1.at[part, col],
        )

    def deliver(part, step):
        target = lax.rem(sub + step, count)
        return pltpu.make_async_remote_copy(
            src_ref=stage.at[target, pl.ds(part * size, size), :],
            dst_ref=out.at[sub, pl.ds(first + part * size, size), :],
            send_sem=send2.at[part, step],
            recv_sem=recv2.at[part, sub],
            device_id=(target, row, col),
            device_id_type=MESH,
        )

    def place(part):
        return pltpu.make_async_copy(
            stage.at[sub, pl.ds(part * size, size), :],
            out.at[sub, pl.ds(first + part * size, size), :],
            recv2.at[part, sub],
        )

    def arrived(ref, sem):
        pltpu.make_async_copy(ref, ref, sem).wait()

    for part in range(chunks):
        for step in range(1, count):
            spread(part, step).start()
        keep(part).start()
    for part in range(chunks):
        for step in list(range(1, count)) + [0]:
            source = lax.rem(sub + step, count)
            arrived(stage.at[source, pl.ds(part * size, size), :], recv1.at[part, source])
            if step:
                deliver(part, step).start()
            else:
                place(part).start()
    for part in range(chunks):
        for source in range(count):
            arrived(out.at[source, pl.ds(first + part * size, size), :], recv2.at[part, source])
        for step in range(1, count):
            spread(part, step).wait_send()
            deliver(part, step).wait_send()


def exchange(child, received, first, rows, chunks, count, ident):
    total, width = child.shape[1], child.shape[2] // count
    aliased = received is not None
    operands = (child, received) if aliased else (child,)
    anywhere = pl.BlockSpec(memory_space=pl.ANY)
    moved = 2 * count * rows * width * 4
    _, result = pl.pallas_call(
        functools.partial(exchange_kernel, count, first, rows, chunks, aliased),
        out_shape=[
            jax.ShapeDtypeStruct((count, rows, width), jnp.float32),
            jax.ShapeDtypeStruct((count, total, width), jnp.float32),
        ],
        in_specs=[anywhere] * len(operands),
        out_specs=[anywhere, anywhere],
        scratch_shapes=[pltpu.SemaphoreType.DMA((chunks, count))] * 4,
        input_output_aliases={1: 1} if aliased else {},
        compiler_params=pltpu.CompilerParams(
            collective_id=ident, has_side_effects=True, vmem_limit_bytes=48 * 2**20
        ),
        cost_estimate=pl.CostEstimate(flops=0, bytes_accessed=40 * moved, transcendentals=0),
    )(*operands)
    return result


def extended_columns(weights, a, front, pieces, column):
    total = front[:, column * BLK : (column + 1) * BLK]
    for s, piece in enumerate(pieces):
        for j in range(2):
            weight = weights[((a * len(pieces) + s) * 3 + column) * 2 + j]
            total = total + weight * piece[0, :, j * BLK : (j + 1) * BLK]
    return total


def strip_kernel(count, where, weights, front, *refs):
    a = pl.program_id(0)
    for column in range(3):
        refs[-1][:, column * BLK : (column + 1) * BLK] = extended_columns(
            weights, a, front, refs[:count], column
        )


def final_kernel(count, panel_blocks, where, weights, front, *refs):
    pieces = refs[:count]
    rows_first, rows_second, cols_factor, out, right, rows_factor = refs[count:]
    group = pl.program_id(0)

    def split(value):
        top = value.astype(jnp.bfloat16)
        return top, (value - top.astype(jnp.float32)).astype(jnp.bfloat16)

    @pl.when(group == 0)
    def _():
        top, rest = split(cols_factor[...])
        right[:, :PANEL] = rest
        right[:, PANEL : 2 * PANEL] = top
        right[:, 2 * PANEL :] = top

    rows_factor[:, : PANEL // 2] = rows_first[...]
    rows_factor[:, PANEL // 2 :] = rows_second[...]
    top, rest = split(rows_factor[...])
    left = jnp.concatenate([top, rest, top], axis=1)
    for column in range(3):
        col_block = where[1] + column
        span = slice(column * BLK, (column + 1) * BLK)
        update = lax.dot_general(
            left, right[span, :], (((1,), (1,)), ((), ())), preferred_element_type=jnp.float32
        )
        for place in range(3):
            a = group * 3 + place
            row_block = where[0] + a
            band = slice(place * BLK, (place + 1) * BLK)
            here = front[band, span]
            for s, piece in enumerate(pieces):
                at = (where[2 + a * count + s] - 2 * group) * BLK
                held = pl.ds(pl.multiple_of(at, BLK), BLK)
                for j in range(2):
                    weight = weights[((a * count + s) * 3 + column) * 2 + j]
                    here = here + weight * piece[0, held, j * BLK : (j + 1) * BLK]
            both = jnp.logical_and(row_block >= panel_blocks, col_block >= panel_blocks)
            out[band, span] = jnp.where(both, here - update[band, :], here)

            @pl.when(jnp.logical_and(row_block >= panel_blocks, col_block < panel_blocks))
            def _():
                source = jnp.minimum(col_block, panel_blocks - 1) * BLK
                out[band, span] = rows_factor[band, pl.ds(pl.multiple_of(source, BLK), BLK)]


def piece_specs(count, offset):
    def one(s):
        return pl.BlockSpec((1, BLK, 2 * BLK), lambda a, where: (s, where[offset + a * count + s], 0))

    return [one(s) for s in range(count)]


def column_factor(panel_t, pivot_inverse):
    return lax.dot_general(
        panel_t,
        pivot_inverse,
        (((0,), (1,)), ((), ())),
        precision=lax.Precision.HIGH,
        preferred_element_type=jnp.float32,
    )


def shards(front_in, child_updates, pattern, child_map, pivot_inverse):
    sub_count = lax.axis_size("sub")
    row_count = lax.axis_size("row")
    col_count = lax.axis_size("col")
    assert sub_count == col_count
    count = sub_count
    groups = sub_count * col_count
    row_id = lax.axis_index("row")
    group_id = lax.axis_index("sub") * col_count + lax.axis_index("col")
    row_blocks = FRONT // BLK // row_count
    col_blocks = FRONT // BLK // groups
    child_rows = CHILD // BLK // row_count
    child_cols = CHILD // BLK // groups
    panel_blocks = PANEL // BLK
    group_cols = col_blocks * BLK
    first_row = row_id * row_blocks
    first_col = group_id * col_blocks
    assert col_blocks == 3 and child_cols == 2

    masks = lax.all_gather(pattern[0].astype(jnp.float32), ("sub", "col"), axis=0, tiled=False)
    masks = masks.reshape(sub_count, col_count, child_rows, CHILD // BLK // col_count)
    masks = masks.transpose(0, 2, 1, 3).reshape(sub_count, child_rows, CHILD // BLK)
    mine = lax.dynamic_slice_in_dim(masks, group_id * child_cols, child_cols, 2)
    rows_map = lax.dynamic_slice_in_dim(child_map, row_id * child_rows, child_rows, 1)
    cols_map = lax.dynamic_slice_in_dim(child_map, group_id * child_cols, child_cols, 1)
    row_at = first_row + jnp.arange(row_blocks, dtype=jnp.int32)
    col_at = first_col + jnp.arange(col_blocks, dtype=jnp.int32)
    row_hit = rows_map[None] == row_at[:, None, None]
    col_hit = cols_map[None] == col_at[:, None, None]
    fallback = (jnp.arange(row_blocks, dtype=jnp.int32) // 3 * 2)[:, None]
    indices = jnp.arange(child_rows, dtype=jnp.int32)
    row_from = jnp.where(
        row_hit.any(2), jnp.sum(jnp.where(row_hit, indices, 0), axis=2), fallback
    ).astype(jnp.int32)
    kept = jnp.sum(jnp.where(row_hit[..., None], mine[None], 0.0), axis=2)
    weights = jnp.where(col_hit[None], kept[:, None], 0.0)
    weights = weights.transpose(0, 2, 1, 3).reshape(-1)
    where = jnp.concatenate(
        [jnp.stack([first_row, first_col]).astype(jnp.int32), row_from.reshape(-1)]
    )

    rows = child_rows * BLK
    head = min(rows, 4 * BLK)
    received = exchange(child_updates, None, 0, head, 2 * head // BLK, count, 0)
    strip_blocks = min(panel_blocks, row_blocks)
    smem = pl.BlockSpec(memory_space=pltpu.SMEM)
    front_spec = pl.BlockSpec((BLK, group_cols), lambda a, where: (a, 0))
    strip = pl.pallas_call(
        functools.partial(strip_kernel, count),
        grid_spec=pltpu.PrefetchScalarGridSpec(
            num_scalar_prefetch=1,
            grid=(strip_blocks,),
            in_specs=[smem, front_spec] + piece_specs(count, 2),
            out_specs=front_spec,
        ),
        out_shape=jax.ShapeDtypeStruct((strip_blocks * BLK, group_cols), jnp.float32),
        cost_estimate=pl.CostEstimate(flops=0, bytes_accessed=20 * 2**20, transcendentals=0),
    )(where, weights, front_in, *([received] * count))
    group_rows = groups // row_count
    left = rows - head
    child = child_updates
    done = head

    def more(received, blocks, ident):
        return exchange(child, received, done, blocks * BLK, 2 * blocks, count, ident)

    if row_count == 2 and strip_blocks == panel_blocks:
        parts = (2, 3, 3, left // BLK - 8)
        child, strip = lax.optimization_barrier((child, strip))
        other = lax.ppermute(strip, "row", [(0, 1)])
        received = more(received, parts[0], 1)
        done += parts[0] * BLK
        other, received = lax.optimization_barrier((other, received))
        cols_factor = column_factor(jnp.where(row_id == 0, strip, other), pivot_inverse)

        deep = group_rows // col_count
        wide = PANEL // 2
        half = (lax.axis_index("sub") // deep != row_id).astype(jnp.int32)
        sent = lax.dynamic_slice_in_dim(cols_factor, half * wide, wide, 1)
        child, sent = lax.optimization_barrier((child, sent))
        along = lax.all_gather(sent, "sub", axis=0, tiled=False)
        received = more(received, parts[1], 2)
        done += parts[1] * BLK
        along, received = lax.optimization_barrier((along, received))

        first = lax.dynamic_slice_in_dim(along, row_id * deep, deep, 0)
        passed = lax.dynamic_slice_in_dim(along, (1 - row_id) * deep, deep, 0)
        child, first, passed = lax.optimization_barrier((child, first, passed))
        second = lax.ppermute(passed, "row", [(0, 1), (1, 0)])
        first = lax.all_gather(first, "col", axis=0, tiled=False).reshape(-1, wide)
        received = more(received, parts[2], 3)
        done += parts[2] * BLK
        second, received = lax.optimization_barrier((second, received))

        child, second = lax.optimization_barrier((child, second))
        second = lax.all_gather(second, "col", axis=0, tiled=False).reshape(-1, wide)
        received = more(received, parts[3], 4)

        def factor_at(group):
            return (group % col_count) * deep + group // col_count

        second_at = 0
    else:
        if left:
            received = more(received, left // BLK, 1)
        span = strip_blocks * BLK
        pieces = [jnp.where(row_id == part, strip, 0.0) for part in range(-(-PANEL // span))]
        panel_t = lax.psum(jnp.concatenate(pieces, axis=0)[:PANEL], "row")
        cols_factor = column_factor(panel_t, pivot_inverse)
        gathered = lax.all_gather(cols_factor, ("sub", "col"), axis=0, tiled=False)
        gathered = lax.dynamic_slice_in_dim(gathered, row_id * group_rows, group_rows, 0)
        first = second = gathered.reshape(-1, PANEL)

        def factor_at(group):
            return group

        second_at = 1

    group_spec = pl.BlockSpec((group_cols, group_cols), lambda a, where: (a, 0))
    group_pieces = [
        pl.BlockSpec((1, 2 * BLK, 2 * BLK), lambda a, where, s=s: (s, a, 0)) for s in range(count)
    ]
    return pl.pallas_call(
        functools.partial(final_kernel, count, panel_blocks),
        grid_spec=pltpu.PrefetchScalarGridSpec(
            num_scalar_prefetch=1,
            grid=(row_blocks // 3,),
            in_specs=[smem, group_spec] + group_pieces
            + [
                pl.BlockSpec((group_cols, PANEL // 2), lambda a, where: (factor_at(a), 0)),
                pl.BlockSpec((group_cols, PANEL // 2), lambda a, where: (factor_at(a), second_at)),
                pl.BlockSpec((group_cols, PANEL), lambda a, where: (0, 0)),
            ],
            out_specs=group_spec,
            scratch_shapes=[
                pltpu.VMEM((group_cols, 3 * PANEL), jnp.bfloat16),
                pltpu.VMEM((group_cols, PANEL), jnp.float32),
            ],
        ),
        out_shape=jax.ShapeDtypeStruct((row_blocks * BLK, group_cols), jnp.float32),
        compiler_params=pltpu.CompilerParams(vmem_limit_bytes=58 * 2**20),
        cost_estimate=pl.CostEstimate(
            flops=6 * row_blocks * BLK * group_cols * PANEL,
            bytes_accessed=100 * 2**20,
            transcendentals=0,
        ),
    )(where, weights, front_in, *([received] * count), first, second, cols_factor)


def solution(mesh):
    in_specs = (P("row", ("sub", "col")), P("sub", "row", "col"), P("sub", "row", "col"), P(), P())
    out_specs = P("row", ("sub", "col"))
    return jax.shard_map(shards, mesh=mesh, in_specs=in_specs, out_specs=out_specs, check_vma=False)
```
